32 devices in a mesh: space: 8 (over z, y), tm: 4 (over x, core).
Axes of the slice: x: 2, y: 2, z: 4, core: 2. Of those that a mesh axis runs over, the one named last changes fastest.
Arguments:
- field: float32 [8192, 8192], P('space', 'tm'), may hold values from -6 to 6
- range_test: float32 [8192, 256], P('tm'), may hold values from -0.0625 to 0.0625
- corange_test: float32 [512, 8192], P(None, 'space'), may hold values from -0.0625 to 0.0625
Outputs:
- left_factor: float32 [8192, 256], P('space')
- right_factor: float32 [256, 8192], P(None, 'tm')
- residual: float32 [8192, 8192], P('space', 'tm')
The draws below stay inside these ranges and needn't reach their ends.
All inputs are finite; a program needn't handle non-finite values.
Results may differ from the reference program's by a relative error of at most 0.00017.
Values sent between devices are 32-bit elements; how exact they have to be, the bound alone decides.
No kernel may reach another device: no remote copies, remote signals or barrier semaphores. Data moves between devices by JAX's collectives and lax.ppermute only.
A program may use at most 128 MiB of HBM per device.

```python
import jax
import jax.numpy as jnp
from jax import lax

RANK = 256
CORANGE = 512
CELLS = 8192
TIMES = 8192


def block_levels(rng, dims, pieces, low, largest):
    factor_of = 1.0
    for dim, parts in pieces:
        steps = jax.random.uniform(jax.random.fold_in(jax.random.fold_in(rng, 6), dim), (parts,), jnp.float32, low / len(pieces), largest / len(pieces))
        factor_of = factor_of * jnp.repeat(jnp.exp(steps), dims[dim] // parts).reshape((-1,) + (1,) * (len(dims) - 1 - dim))
    return factor_of


def scatter_about(rng, shape, spread, reach, shards=(), kind=jnp.bfloat16):
    values = jax.random.normal(rng, shape, jnp.float32) * spread
    if len(shards) > 0:
        values = block_levels(rng, shape, shards, -0.22, 0.18) * values
    return jnp.clip(values, min=-reach, max=reach).astype(kind)


def setup_inputs(seed: int = 0) -> dict:
    splits = jax.random.split(jax.random.key(seed), 4)
    field = scatter_about(splits[0], (CELLS, TIMES), 1.0, 6.0, ((0, 8), (1, 4)), jnp.float32)
    range_test = scatter_about(splits[1], (TIMES, RANK), TIMES ** -0.5, 0.0625, ((0, 4),), jnp.float32)
    corange_test = scatter_about(splits[2], (CORANGE, CELLS), CELLS ** -0.5, 0.0625, ((1, 8),), jnp.float32)
    return dict(field=field, range_test=range_test, corange_test=corange_test)


def product(left, right):
    return jnp.dot(left.astype(jnp.float32), right.astype(jnp.float32), preferred_element_type=jnp.float32, precision=lax.Precision.HIGHEST)

def reference(field, range_test, corange_test):
    sketch = product(field, range_test)
    cosketch = product(corange_test, field)
    gram = product(sketch.T, sketch)
    lower = jnp.linalg.cholesky(gram)
    basis = lax.linalg.triangular_solve(lower, sketch, left_side=False, lower=True, transpose_a=True)
    core = product(corange_test, basis)
    normal = product(core.T, core)
    factor = jnp.linalg.cholesky(normal)
    rhs = product(core.T, cosketch)
    middle = lax.linalg.triangular_solve(factor, rhs, left_side=True, lower=True)
    right_factor = lax.linalg.triangular_solve(factor, middle, left_side=True, lower=True, transpose_a=True)
    residual = field - product(basis, right_factor)
    left_factor = basis * jnp.sqrt(jnp.float32(CELLS))
    return (left_factor, right_factor, residual)
```

```python
import functools

import jax
import jax.numpy as jnp
from jax import lax
from jax.experimental import pallas as pl
from jax.experimental.pallas import tpu as pltpu
from jax.sharding import PartitionSpec as P

F32 = jnp.float32
BF16 = jnp.bfloat16
VMEM = pl.BlockSpec(memory_space=pltpu.VMEM)
SMEM = pl.BlockSpec(memory_space=pltpu.SMEM)
PANEL = 64
PARAMS = pltpu.CompilerParams(vmem_limit_bytes=48 * 2**20)


def exact(a, b, dims):
    return lax.dot_general(
        a, b, (dims, ((), ())), precision=lax.Precision.HIGHEST, preferred_element_type=F32
    )


def split(x):
    hi = x.astype(BF16)
    return hi, (x - hi.astype(F32)).astype(BF16)


def three(a, b, dims=((1,), (0,))):
    def one(x, y):
        return lax.dot_general(x, y, (dims, ((), ())), preferred_element_type=F32)

    return one(a[0], b[0]) + (one(a[0], b[1]) + one(a[1], b[0]))


def cost(macs, moved):
    return pl.CostEstimate(flops=2 * macs, bytes_accessed=moved, transcendentals=0)


def shape(*dims, dtype=F32):
    return jax.ShapeDtypeStruct(dims, dtype)


def sketch_kernel(steps, place, field, test, corange, s_send, s_keep, m_send, m_keep, thi, tlo, total):
    i = pl.program_id(0)

    @pl.when(i == 0)
    def _():
        thi[...], tlo[...] = split(test[...])
        total[...] = jnp.zeros_like(total)

    s = three(split(field[...]), (thi[...], tlo[...]))

    @pl.when(i < steps // 2)
    def _():
        s_send[...] = s

    @pl.when(i >= steps // 2)
    def _():
        s_keep[...] = s

    total[...] += three(split(corange[...]), split(s))

    @pl.when(i == steps - 1)
    def _():
        rows = total.shape[0] // 8
        mine = place[steps]
        for out, slots in ((m_send, (1, 5, 3, 7)), (m_keep, (0, 4, 2, 6))):
            for j, slot in enumerate(slots):
                out[j * rows:(j + 1) * rows, :] = total[pl.ds(pl.multiple_of((mine ^ slot) * rows, 8), rows), :]


def sketches(place, steps, field, test, corange):
    cells, times = field.shape
    rank = test.shape[1]
    rows = cells // steps
    half = steps // 2
    wide = corange.shape[0]
    return pl.pallas_call(
        functools.partial(sketch_kernel, steps),
        grid_spec=pltpu.PrefetchScalarGridSpec(
            num_scalar_prefetch=1,
            grid=(steps,),
            in_specs=[
                pl.BlockSpec((rows, times), lambda i, p: (p[i], 0)),
                pl.BlockSpec((times, rank), lambda i, p: (0, 0)),
                pl.BlockSpec((wide, rows), lambda i, p: (0, p[i])),
            ],
            out_specs=[
                pl.BlockSpec((rows, rank), lambda i, p: (jnp.minimum(i, half - 1), 0)),
                pl.BlockSpec((rows, rank), lambda i, p: (jnp.maximum(i - half, 0), 0)),
                pl.BlockSpec((wide // 2, rank), lambda i, p: (0, 0)),
                pl.BlockSpec((wide // 2, rank), lambda i, p: (0, 0)),
            ],
            scratch_shapes=[
                pltpu.VMEM((times, rank), BF16),
                pltpu.VMEM((times, rank), BF16),
                pltpu.VMEM((wide, rank), F32),
            ],
        ),
        out_shape=[shape(cells // 2, rank)] * 2 + [shape(wide // 2, rank)] * 2,
        compiler_params=PARAMS,
        cost_estimate=cost(3 * cells * rank * (times + wide), 4 * cells * times),
        name="sketches",
    )(place, field, test, corange)


def gram_kernel(core, a, b, s, g_send, g_keep, total):
    x = a[...] + b[...]
    s[...] = x
    total[...] = exact(x, x, ((0,), (0,)))
    rows = total.shape[0] // 2
    me = core[0]
    g_keep[...] = total[pl.ds(pl.multiple_of(me * rows, 8), rows), :]
    g_send[...] = total[pl.ds(pl.multiple_of((1 - me) * rows, 8), rows), :]


def gram_of(core, a, b):
    rank = a.shape[1]
    return pl.pallas_call(
        gram_kernel,
        out_shape=[shape(*a.shape), shape(rank // 2, rank), shape(rank // 2, rank)],
        in_specs=[SMEM, VMEM, VMEM],
        out_specs=[VMEM] * 3,
        scratch_shapes=[pltpu.VMEM((rank, rank), F32)],
        cost_estimate=cost(6 * a.shape[0] * rank * rank, 12 * a.shape[0] * rank),
        name="gram",
    )(core, a, b)


ORDER = (0, 4, 2, 6, 1, 5, 3, 7)


def project_kernel(mine, near, far, corange, normal, phi, plo, m, om):
    half = near.shape[0]
    m[:half] = near[...]
    m[half:] = far[...]
    rows = m.shape[0] // 8
    for j, slot in enumerate(ORDER):
        om[j * rows:(j + 1) * rows, :] = corange[pl.ds(pl.multiple_of((mine[0] ^ slot) * rows, 8), rows), :]
    x = m[...]
    normal[...] = exact(x, x, ((0,), (0,)))
    p = three(split(x.T), split(om[...]))
    phi[...], plo[...] = split(p)


def project(mine, near, far, corange):
    wide, cells = corange.shape
    rank = near.shape[1]
    return pl.pallas_call(
        project_kernel,
        out_shape=[shape(rank, rank), shape(rank, cells, dtype=BF16), shape(rank, cells, dtype=BF16)],
        in_specs=[SMEM, VMEM, VMEM, VMEM],
        out_specs=[VMEM] * 3,
        scratch_shapes=[pltpu.VMEM((wide, rank), F32), pltpu.VMEM((wide, cells), F32)],
        compiler_params=PARAMS,
        cost_estimate=cost(6 * wide * rank * rank + 3 * wide * rank * cells, 4 * wide * cells),
        name="project",
    )(mine, near, far, corange)


def rhs_kernel(place, phi, plo, field, *outs):
    i = pl.program_id(0)
    x = three((phi[...], plo[...]), split(field[...]))
    for k, out in enumerate(outs):
        @pl.when(i == k)
        def _():
            out[...] = x


def rhs_blocks(place, phi, plo, field, count, blocks):
    rank, cells = phi.shape
    cols = field.shape[1] // blocks
    return pl.pallas_call(
        rhs_kernel,
        grid_spec=pltpu.PrefetchScalarGridSpec(
            num_scalar_prefetch=1,
            grid=(count,),
            in_specs=[
                pl.BlockSpec((rank, cells), lambda i, p: (0, 0)),
                pl.BlockSpec((rank, cells), lambda i, p: (0, 0)),
                pl.BlockSpec((cells, cols), lambda i, p: (0, p[i])),
            ],
            out_specs=[pl.BlockSpec((rank, cols), lambda i, p: (0, 0))] * count,
        ),
        out_shape=[shape(rank, cols)] * count,
        compiler_params=PARAMS,
        cost_estimate=cost(3 * count * rank * cells * cols, 4 * count * cells * cols),
        name="rhs",
    )(place, phi, plo, field)


def eliminate(blocks):
    width = blocks[0].shape[1]
    groups = PANEL // 8
    mats = [[x[8 * g:8 * g + 8] for g in range(groups)] for x in blocks]
    row = lax.broadcasted_iota(jnp.int32, (8, width), 0)
    for s in range(groups):
        columns = [
            {
                g: [jnp.broadcast_to(m[g][:, 8 * s + j:8 * s + j + 1], (8, width)) for j in range(8)]
                for g in range(s, groups)
            }
            for m in mats
        ]
        for i in range(8):
            for m, c in zip(mats, columns):
                inverse = 1.0 / c[s][i][i:i + 1]
                below = {g: c[g][i] for g in range(s, groups)}
                below[s] = jnp.where(row > i, below[s], 0.0)
                for j in range(i + 1, 8):
                    f = c[s][j][i:i + 1] * inverse
                    for g in range(s, groups):
                        c[g][j] = c[g][j] - below[g] * f
                u = m[s][i:i + 1] * inverse
                for g in range(s, groups):
                    m[g] = m[g] - below[g] * u
    return mats


def iotas(dims):
    return lax.broadcasted_iota(jnp.int32, dims, 0), lax.broadcasted_iota(jnp.int32, dims, 1)


def factor_both(n, tables):
    r, c = iotas((PANEL, PANEL))
    eye = jnp.where(r == c, 1.0, 0.0)
    r, c = iotas((PANEL, 2 * PANEL))
    for k in range(n // PANEL):
        lo, hi = k * PANEL, (k + 1) * PANEL
        blocks = [jnp.concatenate([t[lo:hi, lo:hi], eye], axis=1) for t in tables]
        left = lo // 128 * 128
        right = n + (hi + 127) // 128 * 128
        rest = hi // 128 * 128
        for t, m in zip(tables, eliminate(blocks)):
            x = jnp.concatenate(m, axis=0)
            pivots = jnp.sum(jnp.where(r == c, x, 0.0), axis=1, keepdims=True)
            inverse = (x * lax.rsqrt(pivots))[:, PANEL:]
            panel = exact(inverse, t[lo:hi, left:right], ((1,), (0,)))
            if hi < n:
                update = exact(panel[:, rest - left:n - left], panel[:, rest - left:], ((0,), (0,)))
                t[hi:n, rest:right] = t[hi:n, rest:right] - update[hi - rest:]
            t[lo:hi, left:right] = panel


def factor_kernel(g_near, g_far, core, normal, upper, inverse, normal_inverse, t1, t2):
    n = normal.shape[0]
    half = n // 2
    r, c = iotas((n, n))
    eye = jnp.where(r == c, 1.0, 0.0)
    me = core[0]
    t1[pl.ds(pl.multiple_of(me * half, 8), half), :n] = g_near[...]
    t1[pl.ds(pl.multiple_of((1 - me) * half, 8), half), :n] = g_far[...]
    t1[:, n:] = eye
    t2[:, :n] = normal[...]
    t2[:, n:] = eye
    factor_both(n, (t1, t2))
    upper[...] = jnp.where(r <= c, t1[:, :n], 0.0)
    inverse[...] = t1[:, n:]
    k = t2[:, n:]
    normal_inverse[...] = exact(k, k, ((0,), (0,)))


def factor(core, g_near, g_far, normal):
    n = normal.shape[0]
    return pl.pallas_call(
        factor_kernel,
        out_shape=[shape(n, n)] * 3,
        in_specs=[VMEM, VMEM, SMEM, VMEM],
        out_specs=[VMEM] * 3,
        scratch_shapes=[pltpu.VMEM((n, 2 * n), F32)] * 2,
        compiler_params=PARAMS,
        cost_estimate=cost(7 * 10**9, 4 * n * n * 8),
        name="factor",
    )(g_near, g_far, core, normal)


def solve_kernel(inverse, *refs):
    total = refs[0][...]
    for ref in refs[1:-1]:
        total += ref[...]
    refs[-1][...] = exact(inverse[...], total, ((1,), (0,)))


def solve(inverse, terms):
    return pl.pallas_call(
        solve_kernel,
        out_shape=shape(*terms[0].shape),
        cost_estimate=cost(6 * inverse.shape[0] * terms[0].size, 4 * terms[0].size * (len(terms) + 2)),
        name="solve",
    )(inverse, *terms)


def output_kernel(count, scale, place, s0, s2, s13, upper, inverse, field, *refs):
    blocks = refs[:count]
    left, right, residual, shi, slo, uhi, ulo, z = refs[count:]
    i = pl.program_id(0)
    rows = s0.shape[0]
    tm = place[count]
    pieces = ((0, s0, 0), (2, s2, 0), (1, s13, 0), (3, s13, rows))

    @pl.when(i == 0)
    def _():
        uhi[...], ulo[...] = split(upper[...])
        inv = split(inverse[...])
        for slot, ref, start in pieces:
            at = pl.ds(pl.multiple_of((tm ^ slot) * rows, 16), rows)
            s = split(ref[start:start + rows, :])
            shi[at, :], slo[at, :] = s
            left[at, :] = three(s, inv, ((1,), (1,))) * scale

    for k in range(count):
        @pl.when(i == k)
        def _():
            z[...] = blocks[k][...]

    zs = split(z[...])
    right[...] = three((uhi[...], ulo[...]), zs)
    residual[...] = field[...] - three((shi[...], slo[...]), zs)


def outputs(place, scale, s0, s2, s13, upper, inverse, field, blocks):
    cells, times = field.shape
    rank, cols = blocks[0].shape
    count = len(blocks)
    whole = lambda *dims: pl.BlockSpec(dims, lambda i, p: (0,) * len(dims))
    return pl.pallas_call(
        functools.partial(output_kernel, count, scale),
        grid_spec=pltpu.PrefetchScalarGridSpec(
            num_scalar_prefetch=1,
            grid=(count,),
            in_specs=[whole(*s0.shape), whole(*s2.shape), whole(*s13.shape), whole(rank, rank), whole(rank, rank),
                      pl.BlockSpec((cells, cols), lambda i, p: (0, p[i]))] + [whole(rank, cols)] * count,
            out_specs=[
                whole(cells, rank),
                pl.BlockSpec((rank, cols), lambda i, p: (0, p[i])),
                pl.BlockSpec((cells, cols), lambda i, p: (0, p[i])),
            ],
            scratch_shapes=[pltpu.VMEM((cells, rank), BF16)] * 2
            + [pltpu.VMEM((rank, rank), BF16)] * 2
            + [pltpu.VMEM((rank, cols), F32)],
        ),
        out_shape=[shape(cells, rank), shape(rank, times), shape(cells, times)],
        compiler_params=PARAMS,
        cost_estimate=cost(3 * cells * rank * times, 8 * cells * times),
        name="outputs",
    )(place, s0, s2, s13, upper, inverse, field, *blocks)


def swap(axis, bit):
    n = lax.axis_size(axis)

    def go(x):
        return lax.ppermute(x, axis, [(i, i ^ bit) for i in range(n)])

    return go


def per_device(field, range_test, corange_test):
    spaces, tms = lax.axis_size("space"), lax.axis_size("tm")
    space, tm = lax.axis_index("space"), lax.axis_index("tm")
    scale = float(field.shape[0] * spaces) ** 0.5
    core, y, x = tm & 1, space & 1, (tm >> 1) & 1
    to_core, to_x = swap("tm", 1), swap("tm", 2)
    to_y = swap("space", 1)

    slots = jnp.array([1, 3, 2, 0], jnp.int32)
    rows_at = ((tm ^ slots)[:, None] * 2 + jnp.arange(2, dtype=jnp.int32)[None, :]).reshape(-1)
    mine = (core | (y << 1) | (x << 2)).astype(jnp.int32)
    place = jnp.concatenate([rows_at.astype(jnp.int32), mine[None]])
    core_at = core.astype(jnp.int32)[None]

    s_send, s_keep, m_send, m_keep = sketches(place, 8, field, range_test, corange_test)
    quarter = s_keep.shape[0] // 2

    m = m_keep + to_core(m_send)
    rows = m.shape[0] // 4
    m = m[:2 * rows] + to_y(m[2 * rows:])
    m = m[:rows] + to_x(m[rows:])
    bit = 2
    while bit < spaces:
        m = m + swap("space", bit)(m)
        bit *= 2
    m = jnp.concatenate([m, to_x(m)], axis=0)
    m = jnp.concatenate([m, to_y(m)], axis=0)
    m_far = to_core(m)

    got = to_core(s_send)
    s_x = to_x(s_keep[:quarter] + got[quarter:])
    s0, g_send, g_keep = gram_of(core_at, s_keep[quarter:] + got[:quarter], s_x)
    g = g_keep + to_core(g_send)
    g = g + to_x(g)
    bit = 1
    while bit < spaces:
        g = g + swap("space", bit)(g)
        bit *= 2
    g_far = to_core(g)

    normal, phi, plo = project(mine[None], m, m_far, corange_test)
    count = min(spaces, 8)
    near = space & (count - 1)
    send_at = (near ^ jnp.arange(count - 1, 0, -2, dtype=jnp.int32)).astype(jnp.int32)
    keep_at = (near ^ jnp.arange(count - 2, -1, -2, dtype=jnp.int32)).astype(jnp.int32)
    sent = rhs_blocks(send_at, phi, plo, field, count // 2, count)
    kept = rhs_blocks(keep_at, phi, plo, field, count // 2, count)
    terms = []
    for k, slot in enumerate(range(count - 2, -1, -2)):
        got = to_y(sent[k])
        if slot == 0:
            terms += [kept[k], got]
        else:
            terms.append(swap("space", slot)(kept[k] + got))

    bit = count
    while bit < spaces:
        mine_sum = functools.reduce(jnp.add, terms)
        terms = [mine_sum, swap("space", bit)(mine_sum)]
        bit *= 2

    upper, inverse, normal_inverse = factor(core_at, g, g_far, normal)
    z0 = solve(normal_inverse, terms)

    s2 = to_x(s0)
    s13 = to_core(jnp.concatenate([s0, s2], axis=0))

    blocks = [None] * count
    blocks[0] = z0
    blocks[1] = to_y(z0)
    for slot in range(2, count, 2):
        blocks[slot] = swap("space", slot)(z0)
    for slot in range(2, count, 2):
        blocks[slot + 1] = to_y(blocks[slot])

    at = jnp.concatenate([(near ^ jnp.arange(count, dtype=jnp.int32)).astype(jnp.int32), tm.astype(jnp.int32)[None]])
    return outputs(at, scale, s0, s2, s13, upper, inverse, field, blocks)


def solution(mesh):
    return jax.shard_map(
        per_device,
        mesh=mesh,
        in_specs=(P("space", "tm"), P("tm", None), P(None, "space")),
        out_specs=(P("space", None), P(None, "tm"), P("space", "tm")),
        check_vma=False,
    )
```

```python
import functools

import jax
import jax.numpy as jnp
from jax import lax
from jax.experimental import pallas as pl
from jax.experimental.pallas import tpu as pltpu
from jax.sharding import PartitionSpec as P

F32 = jnp.float32
BF16 = jnp.bfloat16
VMEM = pl.BlockSpec(memory_space=pltpu.VMEM)
SMEM = pl.BlockSpec(memory_space=pltpu.SMEM)
PANEL = 64
HBM = pl.BlockSpec(memory_space=pltpu.HBM)

CORE, MINE, TM = 8, 9, 10


def params(mib):
    return pltpu.CompilerParams(vmem_limit_bytes=mib * 2**20)


def exact(a, b, dims):
    return lax.dot_general(
        a, b, (dims, ((), ())), precision=lax.Precision.HIGHEST, preferred_element_type=F32
    )


def split(x):
    hi = x.astype(BF16)
    return hi, (x - hi.astype(F32)).astype(BF16)


def three(a, b, dims=((1,), (0,))):
    def one(x, y):
        return lax.dot_general(x, y, (dims, ((), ())), preferred_element_type=F32)

    return one(a[0], b[0]) + (one(a[0], b[1]) + one(a[1], b[0]))


def cost(macs, moved):
    return pl.CostEstimate(flops=macs // 8, bytes_accessed=moved // 16, transcendentals=0)


def pick(table, slots, i):
    step = slots[1] - slots[0] if len(slots) > 1 else 0
    return table[slots[0] + step * i]


def shape(*dims, dtype=F32):
    return jax.ShapeDtypeStruct(dims, dtype)


def sketch_kernel(steps, table, field, test, corange, s_send, s_keep, m_send, m_keep, t, om, thi, tlo, total, sems):
    i = pl.program_id(0)
    rank = t.shape[1]
    rows = field.shape[0]
    copies = (pltpu.make_async_copy(test, t, sems.at[0]), pltpu.make_async_copy(corange, om, sems.at[1]))

    @pl.when(i == 0)
    def _():
        for copy in copies:
            copy.start()
        copies[0].wait()
        thi[...], tlo[...] = split(t[...])
        copies[1].wait()
        total[...] = jnp.zeros_like(total)

    s = three(split(field[...]), (thi[...], tlo[...]))
    half = steps // 2
    at = pl.ds(pl.multiple_of((i % half) * rows, 8), rows)

    @pl.when(i < half)
    def _():
        s_send[at, :] = s

    @pl.when(i >= half)
    def _():
        s_keep[at, :] = s

    slot = jnp.where(i == 0, 1, jnp.where(i == 1, 3, jnp.where(i == 2, 2, 0)))
    here = pl.multiple_of((table[TM] ^ slot) * rows, 128)
    total[...] += three(split(om[:, pl.ds(here, rows)]), split(s))

    @pl.when(i == steps - 1)
    def _():
        part = total.shape[0] // 8
        for out, slots in ((m_send, (1, 5, 3, 7)), (m_keep, (0, 4, 2, 6))):
            for j, k in enumerate(slots):
                from_ = pl.multiple_of((table[MINE] ^ k) * part, 8)
                out[j * part:(j + 1) * part, :] = total[pl.ds(from_, part), :]


def sketches(table, field, test, corange):
    cells, times = field.shape
    rank = test.shape[1]
    steps = 4
    rows = cells // steps
    wide = corange.shape[0]

    def block(i, p):
        return (p[TM] ^ jnp.where(i == 0, 1, jnp.where(i == 1, 3, jnp.where(i == 2, 2, 0))), 0)

    return pl.pallas_call(
        functools.partial(sketch_kernel, steps),
        grid_spec=pltpu.PrefetchScalarGridSpec(
            num_scalar_prefetch=1,
            grid=(steps,),
            in_specs=[pl.BlockSpec((rows, times), block), HBM, HBM],
            out_specs=[VMEM] * 4,
            scratch_shapes=[
                pltpu.VMEM((times, rank), F32),
                pltpu.VMEM((wide, cells), F32),
                pltpu.VMEM((times, rank), BF16),
                pltpu.VMEM((times, rank), BF16),
                pltpu.VMEM((wide, rank), F32),
                pltpu.SemaphoreType.DMA((2,)),
            ],
        ),
        out_shape=[shape(cells // 2, rank)] * 2 + [shape(wide // 2, rank)] * 2,
        compiler_params=params(36),
        cost_estimate=cost(3 * cells * rank * (times + wide), 4 * cells * times),
        name="sketches",
    )(table, field, test, corange)


def gram_kernel(table, a, b, s, g_send, g_keep, total):
    x = a[...] + b[...]
    s[...] = x
    total[...] = exact(x, x, ((0,), (0,)))
    rows = total.shape[0] // 2
    me = table[CORE]
    g_keep[...] = total[pl.ds(pl.multiple_of(me * rows, 8), rows), :]
    g_send[...] = total[pl.ds(pl.multiple_of((1 - me) * rows, 8), rows), :]


def gram_of(table, a, b):
    rank = a.shape[1]
    return pl.pallas_call(
        gram_kernel,
        out_shape=[shape(*a.shape), shape(rank // 2, rank), shape(rank // 2, rank)],
        in_specs=[SMEM, VMEM, VMEM],
        out_specs=[VMEM] * 3,
        scratch_shapes=[pltpu.VMEM((rank, rank), F32)],
        cost_estimate=cost(6 * a.shape[0] * rank * rank, 12 * a.shape[0] * rank),
        name="gram",
    )(table, a, b)


ORDER = (0, 4, 2, 6, 1, 5, 3, 7)


def stack_rows(parts):
    return jnp.concatenate([parts[0], parts[1], parts[0]], axis=0)


def rhs_kernel(slots, first, table, *refs):
    count = len(slots)
    i = pl.program_id(0)
    if first:
        near, far, corange, field = refs[:4]
        outs, (p, m, om) = refs[4:-3], refs[-3:]

        @pl.when(i == 0)
        def _():
            half = near.shape[0]
            rows = half // 4
            m[:half] = near[...]
            m[half:] = far[...]
            for j, slot in enumerate(ORDER):
                at = pl.multiple_of((table[MINE] ^ slot) * rows, 8)
                om[j * rows:(j + 1) * rows, :] = corange[pl.ds(at, rows), :]
            cells = om.shape[1]
            p[:, :cells], p[:, 2 * cells:] = split(three(split(m[...].T), split(om[...])))
            p[:, cells:2 * cells] = p[:, :cells]
    else:
        p, field = refs[:2]
        outs = refs[2:]
    x = jnp.dot(p[...], stack_rows(split(field[...])), preferred_element_type=F32)
    for k in range(count):
        @pl.when(i == k)
        def _():
            outs[k][...] = x


def rhs_blocks(table, slots, operands, field, blocks):
    count = len(slots)
    first = len(operands) > 1
    rank = operands[0].shape[1] if first else operands[0].shape[0]
    cells = field.shape[0]
    cols = field.shape[1] // blocks
    wide = operands[2].shape[0] if first else 0
    whole = lambda dims: pl.BlockSpec(dims, lambda i, p: (0, 0))
    return pl.pallas_call(
        functools.partial(rhs_kernel, slots, first),
        grid_spec=pltpu.PrefetchScalarGridSpec(
            num_scalar_prefetch=1,
            grid=(count,),
            in_specs=[whole(x.shape) for x in operands] + [pl.BlockSpec((cells, cols), lambda i, p: (0, pick(p, slots, i)))],
            out_specs=[whole((rank, cols))] * count + [whole((rank, 3 * cells))] * first,
            scratch_shapes=[pltpu.VMEM((wide, rank), F32), pltpu.VMEM((wide, cells), F32)] * first,
        ),
        out_shape=[shape(rank, cols)] * count + [shape(rank, 3 * cells, dtype=BF16)] * first,
        compiler_params=params(32),
        cost_estimate=cost(3 * count * rank * cells * cols, 4 * count * cells * cols),
        name="rhs",
    )(table, *operands, field)


def eliminate(blocks):
    width = blocks[0].shape[1]
    groups = PANEL // 8
    mats = [[x[8 * g:8 * g + 8] for g in range(groups)] for x in blocks]
    row = lax.broadcasted_iota(jnp.int32, (8, width), 0)
    for s in range(groups):
        columns = [
            {
                g: [jnp.broadcast_to(m[g][:, 8 * s + j:8 * s + j + 1], (8, width)) for j in range(8)]
                for g in range(s, groups)
            }
            for m in mats
        ]
        for i in range(8):
            for m, c in zip(mats, columns):
                inverse = 1.0 / c[s][i][i:i + 1]
                below = {g: c[g][i] for g in range(s, groups)}
                below[s] = jnp.where(row > i, below[s], 0.0)
                for j in range(i + 1, 8):
                    f = c[s][j][i:i + 1] * inverse
                    for g in range(s, groups):
                        c[g][j] = c[g][j] - below[g] * f
                u = m[s][i:i + 1] * inverse
                for g in range(s, groups):
                    m[g] = m[g] - below[g] * u
    return mats


def iotas(dims):
    return lax.broadcasted_iota(jnp.int32, dims, 0), lax.broadcasted_iota(jnp.int32, dims, 1)


def factor_both(n, tables):
    r, c = iotas((PANEL, PANEL))
    eye = jnp.where(r == c, 1.0, 0.0)
    r, c = iotas((PANEL, 2 * PANEL))
    for k in range(n // PANEL):
        lo, hi = k * PANEL, (k + 1) * PANEL
        blocks = [jnp.concatenate([t[lo:hi, lo:hi], eye], axis=1) for t in tables]
        left = lo // 128 * 128
        right = n + (hi + 127) // 128 * 128
        rest = hi // 128 * 128
        for t, m in zip(tables, eliminate(blocks)):
            x = jnp.concatenate(m, axis=0)
            pivots = jnp.sum(jnp.where(r == c, x, 0.0), axis=1, keepdims=True)
            inverse = (x * lax.rsqrt(pivots))[:, PANEL:]
            panel = exact(inverse, t[lo:hi, left:right], ((1,), (0,)))
            if hi < n:
                update = exact(panel[:, rest - left:n - left], panel[:, rest - left:], ((0,), (0,)))
                t[hi:n, rest:right] = t[hi:n, rest:right] - update[hi - rest:]
            t[lo:hi, left:right] = panel


def factor_kernel(table, g_near, g_far, m_near, m_far, upper, inverse, normal_inverse, t1, t2):
    n = g_near.shape[1]
    half = n // 2
    r, c = iotas((n, n))
    eye = jnp.where(r == c, 1.0, 0.0)
    me = table[CORE]
    t1[pl.ds(pl.multiple_of(me * half, 8), half), :n] = g_near[...]
    t1[pl.ds(pl.multiple_of((1 - me) * half, 8), half), :n] = g_far[...]
    t1[:, n:] = eye
    t2[:, :n] = exact(m_near[...], m_near[...], ((0,), (0,))) + exact(m_far[...], m_far[...], ((0,), (0,)))
    t2[:, n:] = eye
    factor_both(n, (t1, t2))
    upper[...] = jnp.where(r <= c, t1[:, :n], 0.0)
    inverse[...] = t1[:, n:]
    k = t2[:, n:]
    normal_inverse[...] = exact(k, k, ((0,), (0,)))


def factor(table, g_near, g_far, m_near, m_far):
    n = g_near.shape[1]
    return pl.pallas_call(
        factor_kernel,
        out_shape=[shape(n, n)] * 3,
        in_specs=[SMEM] + [VMEM] * 4,
        out_specs=[VMEM] * 3,
        scratch_shapes=[pltpu.VMEM((n, 2 * n), F32)] * 2,
        compiler_params=params(20),
        cost_estimate=cost(5 * 10**9, 4 * n * n * 8),
        name="factor",
    )(table, g_near, g_far, m_near, m_far)


def solve_kernel(projector, *refs):
    total = refs[0][...]
    for ref in refs[1:-1]:
        total += ref[...]
    refs[-1][...] = three(split(projector[...]), split(total))


def solve(projector, terms):
    return pl.pallas_call(
        solve_kernel,
        out_shape=shape(projector.shape[0], terms[0].shape[1]),
        in_specs=[VMEM] * (len(terms) + 1),
        out_specs=VMEM,
        compiler_params=params(16),
        cost_estimate=cost(3 * projector.shape[0] * terms[0].size, 4 * terms[0].size * (len(terms) + 2)),
        name="solve",
    )(projector, *terms)


def output_kernel(slots, scale, table, *refs):
    count = len(slots)
    first = scale is not None
    i = pl.program_id(0)
    if first:
        s0, s2, s13, upper, inverse, field = refs[:6]
        blocks = refs[6:6 + count]
        left, sparts, uparts, right, residual, z = refs[6 + count:]
        rows, rank = s0.shape

        @pl.when(i == 0)
        def _():
            uparts[:, :rank], uparts[:, 2 * rank:] = split(upper[...])
            uparts[:, rank:2 * rank] = uparts[:, :rank]
            inv = split(inverse[...])
            for slot, ref, start in ((0, s0, 0), (2, s2, 0), (1, s13, 0), (3, s13, rows)):
                at = pl.ds(pl.multiple_of((table[TM] ^ slot) * rows, 16), rows)
                hi, lo = split(ref[start:start + rows, :])
                sparts[at, :rank] = hi
                sparts[at, rank:2 * rank] = hi
                sparts[at, 2 * rank:] = lo
                left[at, :] = three((hi, lo), inv, ((1,), (1,))) * scale
    else:
        sparts, uparts, field = refs[:3]
        blocks = refs[3:3 + count]
        right, residual, z = refs[5 + count:]

    for k in range(count):
        @pl.when(i == k)
        def _():
            z[...] = stack_rows(split(blocks[k][...]))

    right[...] = jnp.dot(uparts[...], z[...], preferred_element_type=F32)
    residual[...] = field[...] - jnp.dot(sparts[...], z[...], preferred_element_type=F32)


def outputs(table, slots, scale, operands, field, blocks, before=()):
    cells, times = field.shape
    rank, cols = blocks[0].shape
    count = len(slots)
    first = scale is not None
    whole = lambda *dims: pl.BlockSpec(dims, lambda i, p: (0,) * len(dims))
    ahead = 1 + len(operands) + 1 + count
    return pl.pallas_call(
        functools.partial(output_kernel, slots, scale),
        grid_spec=pltpu.PrefetchScalarGridSpec(
            num_scalar_prefetch=1,
            grid=(count,),
            in_specs=[whole(*x.shape) for x in operands]
            + [pl.BlockSpec((cells, cols), lambda i, p: (0, pick(p, slots, i)))]
            + [whole(rank, cols)] * count
            + [pl.BlockSpec(memory_space=pl.ANY)] * len(before),
            out_specs=[whole(cells, rank), whole(cells, 3 * rank), whole(rank, 3 * rank)] * first + [
                pl.BlockSpec((rank, cols), lambda i, p: (0, pick(p, slots, i))),
                pl.BlockSpec((cells, cols), lambda i, p: (0, pick(p, slots, i))),
            ],
            scratch_shapes=[pltpu.VMEM((3 * rank, cols), BF16)],
        ),
        out_shape=[shape(cells, rank), shape(cells, 3 * rank, dtype=BF16), shape(rank, 3 * rank, dtype=BF16)] * first
        + [shape(rank, times), shape(cells, times)],
        input_output_aliases={} if first else {ahead: 0, ahead + 1: 1},
        compiler_params=params(36),
        cost_estimate=cost(3 * cells * rank * cols * count, 8 * cells * cols * count),
        name="outputs",
    )(table, *operands, field, *blocks, *before)


def swap(axis, bit):
    n = lax.axis_size(axis)

    def go(x):
        return lax.ppermute(x, axis, [(i, i ^ bit) for i in range(n)])

    return go


def tie(*arrays):
    return lax.optimization_barrier(arrays)


def along_z(v):
    spaces = lax.axis_size("space")
    bit = 2
    if spaces >= 8:
        v = (v + swap("space", 2)(v)) + (swap("space", 4)(v) + swap("space", 6)(v))
        bit = 8
    while bit < spaces:
        v = v + swap("space", bit)(v)
        bit *= 2
    return v


def per_device(field, range_test, corange_test):
    spaces, tms = lax.axis_size("space"), lax.axis_size("tm")
    space, tm = lax.axis_index("space"), lax.axis_index("tm")
    scale = float(field.shape[0] * spaces) ** 0.5
    core, y, x = tm & 1, space & 1, (tm >> 1) & 1
    to_core, to_x = swap("tm", 1), swap("tm", 2)
    to_y = swap("space", 1)

    def to_xy(v):
        pairs = [(s * tms + t, (s ^ 1) * tms + (t ^ 2)) for s in range(spaces) for t in range(tms)]
        return lax.ppermute(v, ("space", "tm"), pairs)


    count = min(spaces, 8)
    near = space & (count - 1)
    mine = core | (y << 1) | (x << 2)
    numbers = jnp.array([core, mine, tm])
    table = jnp.concatenate([near ^ jnp.arange(8, dtype=jnp.int32), numbers]).astype(jnp.int32)

    s_send, s_keep, m_send, m_keep = sketches(table, field, range_test, corange_test)
    quarter = s_keep.shape[0] // 2

    m = m_keep + to_core(m_send)
    got = to_core(s_send)
    s_far, s_near = s_keep[:quarter] + got[quarter:], s_keep[quarter:] + got[:quarter]
    m, s_far, s_near = tie(m, s_far, s_near)
    rows = m.shape[0] // 4
    k0, kx, ky, kxy = (m[i * rows:(i + 1) * rows] for i in range(4))
    s_x = to_x(s_far)
    m = (k0 + to_x(kx)) + (to_y(ky) + to_xy(kxy))
    m, s_x = tie(m, s_x)
    s0, g_send, g = gram_of(table, s_near, s_x)
    g_got = to_core(g_send)
    m = along_z(m)
    m, g, g_got = tie(m, g, g_got)
    g = g + g_got
    g_got = to_x(g)
    m = jnp.concatenate([m, to_x(m), to_y(m), to_xy(m)], axis=0)
    m, g, g_got = tie(m, g, g_got)
    g = g + g_got
    m_far = to_core(m)
    g_got = to_y(g)

    send_slots, keep_slots = list(range(count - 1, 0, -2)), list(range(count - 2, -1, -2))
    cut = (len(send_slots) + 1) // 2
    *sent, p = rhs_blocks(table, send_slots[:cut], (m, m_far, corange_test), field, count)
    p, g, g_got = tie(p, g, g_got)
    g = along_z(g + g_got)
    if send_slots[cut:]:
        sent += rhs_blocks(table, send_slots[cut:], (p,), field, count)
    kept = list(rhs_blocks(table, keep_slots, (p,), field, count))
    terms = []
    for k, slot in enumerate(keep_slots):
        got = to_y(sent[k])
        if slot == 0:
            terms += [kept[k], got]
        else:
            total = kept[k] + got
            if k == 0:
                total, g = tie(total, g)
            terms.append(swap("space", slot)(total))
    bit = count
    while bit < spaces:
        mine_sum = functools.reduce(jnp.add, terms)
        terms = [mine_sum, swap("space", bit)(mine_sum)]
        bit *= 2
    g_far = to_core(g)
    s2 = to_x(s0)
    s13 = to_core(jnp.concatenate([s0, s2], axis=0))

    upper, inverse, inverse_normal = factor(table, g, g_far, m, m_far)
    z0 = solve(inverse_normal, terms)

    blocks = {0: z0, 1: to_y(z0)}
    for slot in range(2, count, 2):
        blocks[slot] = swap("space", slot)(z0)
    for slot in range(2, count, 2):
        blocks[slot + 1] = to_y(blocks[slot])

    left, sparts, uparts, *done = outputs(
        table, [0, 1, 2][:count], scale, (s0, s2, s13, upper, inverse), field, [blocks[k] for k in range(min(3, count))])
    for slots in ([4, 6], [3, 5, 7]):
        if count > slots[-1]:
            done = outputs(table, slots, None, (sparts, uparts), field, [blocks[k] for k in slots], tuple(done))
    return (left, *done)


def solution(mesh):
    return jax.shard_map(
        per_device,
        mesh=mesh,
        in_specs=(P("space", "tm"), P("tm", None), P(None, "space")),
        out_specs=(P("space", None), P(None, "tm"), P("space", "tm")),
        check_vma=False,
    )
```

```python
import functools

import jax
import jax.numpy as jnp
from jax import lax
from jax.experimental import pallas as pl
from jax.experimental.pallas import tpu as pltpu
from jax.sharding import PartitionSpec as P

F32 = jnp.float32
BF16 = jnp.bfloat16
VMEM = pl.BlockSpec(memory_space=pltpu.VMEM)
SMEM = pl.BlockSpec(memory_space=pltpu.SMEM)
PANEL = 64
HBM = pl.BlockSpec(memory_space=pltpu.HBM)

CORE, MINE, TM = 8, 9, 10


def params(mib):
    return pltpu.CompilerParams(vmem_limit_bytes=mib * 2**20)


def exact(a, b, dims):
    return lax.dot_general(
        a, b, (dims, ((), ())), precision=lax.Precision.HIGHEST, preferred_element_type=F32
    )


def split(x):
    hi = x.astype(BF16)
    return hi, (x - hi.astype(F32)).astype(BF16)


def three(a, b, dims=((1,), (0,))):
    def one(x, y):
        return lax.dot_general(x, y, (dims, ((), ())), preferred_element_type=F32)

    return one(a[0], b[0]) + (one(a[0], b[1]) + one(a[1], b[0]))


def cost(macs, moved):
    return pl.CostEstimate(flops=macs // 8, bytes_accessed=moved // 16, transcendentals=0)


def pick(table, slots, i):
    slot = slots[-1]
    for k in range(len(slots) - 1):
        slot = jnp.where(i == k, slots[k], slot)
    return table[slot]


def shape(*dims, dtype=F32):
    return jax.ShapeDtypeStruct(dims, dtype)


def sketch_kernel(table, field, test, corange, s_send, s_keep, m_send, m_keep, fhi, flo, f, t, om, total, sems):
    cells, times = field.shape
    steps = f.shape[0]
    rows = cells // steps
    starts = [pl.multiple_of((table[TM] ^ slot) * rows, 128) for slot in (1, 3, 2, 0)]
    first = pltpu.make_async_copy(test, t, sems.at[steps])
    second = pltpu.make_async_copy(corange, om, sems.at[steps + 1])
    blocks = [pltpu.make_async_copy(field.at[pl.ds(at, rows), :], f.at[i], sems.at[i]) for i, at in enumerate(starts)]
    first.start()
    blocks[0].start()
    second.start()
    for block in blocks[1:]:
        block.start()
    first.wait()
    right = split(t[...])
    for i, at in enumerate(starts):
        blocks[i].wait()
        left = split(f[i])
        fhi[pl.ds(at, rows), :], flo[pl.ds(at, rows), :] = left
        s = three(left, right)
        out, half = (s_send, s_keep)[i // 2], i % 2
        out[half * rows:(half + 1) * rows, :] = s
        if i == 0:
            second.wait()
        part = three(split(om[:, pl.ds(at, rows)]), split(s))
        if i == 0:
            total[...] = part
        else:
            total[...] += part
    part = total.shape[0] // 8
    for out, slots in ((m_send, (1, 5, 3, 7)), (m_keep, (0, 4, 2, 6))):
        for j, k in enumerate(slots):
            at = pl.multiple_of((table[MINE] ^ k) * part, 8)
            out[j * part:(j + 1) * part, :] = total[pl.ds(at, part), :]


def sketches(table, field, test, corange):
    cells, times = field.shape
    rank = test.shape[1]
    steps = 4
    wide = corange.shape[0]
    anywhere = pl.BlockSpec(memory_space=pl.ANY)
    return pl.pallas_call(
        sketch_kernel,
        in_specs=[SMEM] + [anywhere] * 3,
        out_specs=[VMEM] * 6,
        scratch_shapes=[
            pltpu.VMEM((steps, cells // steps, times), F32),
            pltpu.VMEM((times, rank), F32),
            pltpu.VMEM((wide, cells), F32),
            pltpu.VMEM((wide, rank), F32),
            pltpu.SemaphoreType.DMA((steps + 2,)),
        ],
        out_shape=[shape(cells // 2, rank)] * 2 + [shape(wide // 2, rank)] * 2 + [shape(cells, times, dtype=BF16)] * 2,
        compiler_params=params(52),
        cost_estimate=cost(3 * cells * rank * (times + wide), 4 * cells * times),
        name="sketches",
    )(table, field, test, corange)


def gram_kernel(table, a, b, s, g_send, g_keep, total):
    x = a[...] + b[...]
    s[...] = x
    total[...] = exact(x, x, ((0,), (0,)))
    rows = total.shape[0] // 2
    me = table[CORE]
    g_keep[...] = total[pl.ds(pl.multiple_of(me * rows, 8), rows), :]
    g_send[...] = total[pl.ds(pl.multiple_of((1 - me) * rows, 8), rows), :]


def gram_of(table, a, b):
    rank = a.shape[1]
    return pl.pallas_call(
        gram_kernel,
        out_shape=[shape(*a.shape), shape(rank // 2, rank), shape(rank // 2, rank)],
        in_specs=[SMEM, VMEM, VMEM],
        out_specs=[VMEM] * 3,
        scratch_shapes=[pltpu.VMEM((rank, rank), F32)],
        compiler_params=params(8),
        cost_estimate=cost(6 * a.shape[0] * rank * rank, 12 * a.shape[0] * rank),
        name="gram",
    )(table, a, b)


ORDER = (0, 4, 2, 6, 1, 5, 3, 7)


def stack_rows(parts):
    return jnp.concatenate([parts[0], parts[1], parts[0]], axis=0)


def rhs_kernel(slots, first, table, *refs):
    if first:
        near, far, corange, fhi, flo = refs[:5]
        outs, (phi, plo, m, om) = refs[5:-4], refs[-4:]
        half = near.shape[0]
        rows = half // 4
        m[:half] = near[...]
        m[half:] = far[...]
        for j, slot in enumerate(ORDER):
            at = pl.multiple_of((table[MINE] ^ slot) * rows, 8)
            om[j * rows:(j + 1) * rows, :] = corange[pl.ds(at, rows), :]
        phi[...], plo[...] = split(three(split(m[...].T), split(om[...])))
    else:
        phi, plo, fhi, flo = refs[:4]
        outs = refs[4:]
    cols = outs[0].shape[1]
    for k, slot in enumerate(slots):
        at = pl.ds(pl.multiple_of(table[slot] * cols, 128), cols)
        outs[k][...] = three((phi[...], plo[...]), (fhi[:, at], flo[:, at]))


def rhs_blocks(table, slots, operands, parts, blocks):
    count = len(slots)
    first = len(operands) > 2
    rank = operands[0].shape[1] if first else operands[0].shape[0]
    cells, times = parts[0].shape
    cols = times // blocks
    wide = operands[2].shape[0] if first else 0
    return pl.pallas_call(
        functools.partial(rhs_kernel, slots, first),
        in_specs=[SMEM] + [VMEM] * (len(operands) + 2),
        out_specs=[VMEM] * (count + 2 * first),
        scratch_shapes=[pltpu.VMEM((wide, rank), F32), pltpu.VMEM((wide, cells), F32)] * first,
        out_shape=[shape(rank, cols)] * count + [shape(rank, cells, dtype=BF16)] * (2 * first),
        compiler_params=params(20),
        cost_estimate=cost(3 * count * rank * cells * cols, 4 * count * cells * cols),
        name="rhs",
    )(table, *operands, *parts)


def eliminate(blocks):
    width = blocks[0].shape[1]
    groups = PANEL // 8
    mats = [[x[8 * g:8 * g + 8] for g in range(groups)] for x in blocks]
    row = lax.broadcasted_iota(jnp.int32, (8, width), 0)
    for s in range(groups):
        columns = [
            {
                g: [jnp.broadcast_to(m[g][:, 8 * s + j:8 * s + j + 1], (8, width)) for j in range(8)]
                for g in range(s, groups)
            }
            for m in mats
        ]
        for i in range(8):
            for m, c in zip(mats, columns):
                inverse = 1.0 / c[s][i][i:i + 1]
                below = {g: c[g][i] for g in range(s, groups)}
                below[s] = jnp.where(row > i, below[s], 0.0)
                for j in range(i + 1, 8):
                    f = c[s][j][i:i + 1] * inverse
                    for g in range(s, groups):
                        c[g][j] = c[g][j] - below[g] * f
                u = m[s][i:i + 1] * inverse
                for g in range(s, groups):
                    m[g] = m[g] - below[g] * u
    return mats


def iotas(dims):
    return lax.broadcasted_iota(jnp.int32, dims, 0), lax.broadcasted_iota(jnp.int32, dims, 1)


def factor_both(n, tables, panels):
    r, c = iotas((PANEL, PANEL))
    eye = jnp.where(r == c, 1.0, 0.0)
    r, c = iotas((PANEL, 2 * PANEL))
    for k in panels:
        lo, hi = k * PANEL, (k + 1) * PANEL
        blocks = [jnp.concatenate([t[lo:hi, lo:hi], eye], axis=1) for t in tables]
        left = lo // 128 * 128
        right = n + (hi + 127) // 128 * 128
        rest = hi // 128 * 128
        for t, m in zip(tables, eliminate(blocks)):
            x = jnp.concatenate(m, axis=0)
            pivots = jnp.sum(jnp.where(r == c, x, 0.0), axis=1, keepdims=True)
            inverse = (x * lax.rsqrt(pivots))[:, PANEL:]
            panel = exact(inverse, t[lo:hi, left:right], ((1,), (0,)))
            if hi < n:
                update = exact(panel[:, rest - left:n - left], panel[:, rest - left:], ((0,), (0,)))
                t[hi:n, rest:right] = t[hi:n, rest:right] - update[hi - rest:]
            t[lo:hi, left:right] = panel


def factor_head(panels, table, g_near, g_far, m_near, m_far, t1, t2):
    n = g_near.shape[1]
    half = n // 2
    r, c = iotas((n, n))
    eye = jnp.where(r == c, 1.0, 0.0)
    me = table[CORE]
    t1[pl.ds(pl.multiple_of(me * half, 8), half), :n] = g_near[...]
    t1[pl.ds(pl.multiple_of((1 - me) * half, 8), half), :n] = g_far[...]
    t1[:, n:] = eye
    t2[:, :n] = exact(m_near[...], m_near[...], ((0,), (0,))) + exact(m_far[...], m_far[...], ((0,), (0,)))
    t2[:, n:] = eye
    factor_both(n, (t1, t2), panels)


def factor_tail(panels, head1, head2, upper, inverse, normal_inverse, t1, t2):
    n = upper.shape[0]
    t1[...] = head1[...]
    t2[...] = head2[...]
    factor_both(n, (t1, t2), panels)
    r, c = iotas((n, n))
    upper[...] = jnp.where(r <= c, t1[:, :n], 0.0)
    inverse[...] = t1[:, n:]
    k = t2[:, n:]
    normal_inverse[...] = exact(k, k, ((0,), (0,)))


def factor_start(table, g_near, g_far, m_near, m_far):
    n = g_near.shape[1]
    return pl.pallas_call(
        functools.partial(factor_head, range(n // PANEL // 2)),
        out_shape=[shape(n, 2 * n)] * 2,
        in_specs=[SMEM] + [VMEM] * 4,
        out_specs=[VMEM] * 2,
        compiler_params=params(16),
        cost_estimate=cost(3 * 10**9, 4 * n * n * 8),
        name="factor",
    )(table, g_near, g_far, m_near, m_far)


def factor_end(t1, t2):
    n = t1.shape[0]
    return pl.pallas_call(
        functools.partial(factor_tail, range(n // PANEL // 2, n // PANEL)),
        out_shape=[shape(n, n)] * 3,
        in_specs=[VMEM] * 2,
        out_specs=[VMEM] * 3,
        scratch_shapes=[pltpu.VMEM((n, 2 * n), F32)] * 2,
        compiler_params=params(16),
        cost_estimate=cost(3 * 10**9, 4 * n * n * 8),
        name="factor",
    )(t1, t2)


def solve_kernel(projector, *refs):
    total = refs[0][...]
    for ref in refs[1:-1]:
        total += ref[...]
    refs[-1][...] = three(split(projector[...]), split(total))


def solve(projector, terms):
    return pl.pallas_call(
        solve_kernel,
        out_shape=shape(projector.shape[0], terms[0].shape[1]),
        in_specs=[VMEM] * (len(terms) + 1),
        out_specs=VMEM,
        compiler_params=params(16),
        cost_estimate=cost(3 * projector.shape[0] * terms[0].size, 4 * terms[0].size * (len(terms) + 2)),
        name="solve",
    )(projector, *terms)


def output_kernel(slots, scale, table, *refs):
    count = len(slots)
    first = scale is not None
    i = pl.program_id(0)
    if first:
        s0, s2, s13, upper, inverse, field = refs[:6]
        blocks = refs[6:6 + count]
        left, sparts, uparts, right, residual, z = refs[6 + count:]
        rows, rank = s0.shape

        @pl.when(i == 0)
        def _():
            uparts[:, :rank], uparts[:, 2 * rank:] = split(upper[...])
            uparts[:, rank:2 * rank] = uparts[:, :rank]
            inv = split(inverse[...])
            for slot, ref, start in ((0, s0, 0), (2, s2, 0), (1, s13, 0), (3, s13, rows)):
                at = pl.ds(pl.multiple_of((table[TM] ^ slot) * rows, 16), rows)
                hi, lo = split(ref[start:start + rows, :])
                sparts[at, :rank] = hi
                sparts[at, rank:2 * rank] = hi
                sparts[at, 2 * rank:] = lo
                left[at, :] = three((hi, lo), inv, ((1,), (1,))) * scale
    else:
        sparts, uparts, field = refs[:3]
        blocks = refs[3:3 + count]
        right, residual, z = refs[5 + count:]

    for k in range(count):
        @pl.when(i == k)
        def _():
            z[...] = stack_rows(split(blocks[k][...]))

    right[...] = jnp.dot(uparts[...], z[...], preferred_element_type=F32)
    residual[...] = field[...] - jnp.dot(sparts[...], z[...], preferred_element_type=F32)


def outputs(table, slots, scale, operands, field, blocks, before=()):
    cells, times = field.shape
    rank, cols = blocks[0].shape
    count = len(slots)
    first = scale is not None
    whole = lambda *dims: pl.BlockSpec(dims, lambda i, p: (0,) * len(dims))
    ahead = 1 + len(operands) + 1 + count
    return pl.pallas_call(
        functools.partial(output_kernel, slots, scale),
        grid_spec=pltpu.PrefetchScalarGridSpec(
            num_scalar_prefetch=1,
            grid=(count,),
            in_specs=[whole(*x.shape) for x in operands]
            + [pl.BlockSpec((cells, cols), lambda i, p: (0, pick(p, slots, i)))]
            + [whole(rank, cols)] * count
            + [pl.BlockSpec(memory_space=pl.ANY)] * len(before),
            out_specs=[whole(cells, rank), whole(cells, 3 * rank), whole(rank, 3 * rank)] * first + [
                pl.BlockSpec((rank, cols), lambda i, p: (0, pick(p, slots, i))),
                pl.BlockSpec((cells, cols), lambda i, p: (0, pick(p, slots, i))),
            ],
            scratch_shapes=[pltpu.VMEM((3 * rank, cols), BF16)],
        ),
        out_shape=[shape(cells, rank), shape(cells, 3 * rank, dtype=BF16), shape(rank, 3 * rank, dtype=BF16)] * first
        + [shape(rank, times), shape(cells, times)],
        input_output_aliases={} if first else {ahead: 0, ahead + 1: 1},
        compiler_params=params(36),
        cost_estimate=cost(3 * cells * rank * cols * count, 8 * cells * cols * count),
        name="outputs",
    )(table, *operands, field, *blocks, *before)


def swap(axis, bit):
    n = lax.axis_size(axis)

    def go(x):
        return lax.ppermute(x, axis, [(i, i ^ bit) for i in range(n)])

    return go


def tie(*arrays):
    return lax.optimization_barrier(arrays)


def z_parts(v):
    return [v] + [swap("space", bit)(v) for bit in (2, 4, 6)] if lax.axis_size("space") >= 8 else [v]


def z_sum(parts):
    spaces = lax.axis_size("space")
    v, bit = parts[0], 2
    if len(parts) > 1:
        v, bit = (v + parts[1]) + (parts[2] + parts[3]), 8
    while bit < spaces:
        v = v + swap("space", bit)(v)
        bit *= 2
    return v


def per_device(field, range_test, corange_test):
    spaces, tms = lax.axis_size("space"), lax.axis_size("tm")
    space, tm = lax.axis_index("space"), lax.axis_index("tm")
    scale = float(field.shape[0] * spaces) ** 0.5
    core, y, x = tm & 1, space & 1, (tm >> 1) & 1
    to_core, to_x = swap("tm", 1), swap("tm", 2)
    to_y = swap("space", 1)

    def to_xy(v):
        pairs = [(s * tms + t, (s ^ 1) * tms + (t ^ 2)) for s in range(spaces) for t in range(tms)]
        return lax.ppermute(v, ("space", "tm"), pairs)


    count = min(spaces, 8)
    near = space & (count - 1)
    mine = core | (y << 1) | (x << 2)
    numbers = jnp.array([core, mine, tm])
    table = jnp.concatenate([near ^ jnp.arange(8, dtype=jnp.int32), numbers]).astype(jnp.int32)

    s_send, s_keep, m_send, m_keep, *parts = sketches(table, field, range_test, corange_test)
    quarter = s_keep.shape[0] // 2

    m = m_keep + to_core(m_send)
    got = to_core(s_send)
    s_far, s_near = s_keep[:quarter] + got[quarter:], s_keep[quarter:] + got[:quarter]
    m, s_far, s_near = tie(m, s_far, s_near)
    rows = m.shape[0] // 4
    k0, kx, ky, kxy = (m[i * rows:(i + 1) * rows] for i in range(4))
    s_x = to_x(s_far)
    m = (k0 + to_x(kx)) + (to_y(ky) + to_xy(kxy))
    m, s_x = tie(m, s_x)
    s0, g_send, g = gram_of(table, s_near, s_x)
    g_got = to_core(g_send)
    m = z_sum(z_parts(m))
    m, g, g_got = tie(m, g, g_got)
    g = g + g_got
    g_got = to_x(g)
    m = jnp.concatenate([m, to_x(m), to_y(m), to_xy(m)], axis=0)
    m, g, g_got = tie(m, g, g_got)
    g = g + g_got
    m_far = to_core(m)
    g_got = to_y(g)

    send_slots, keep_slots = list(range(count - 1, 0, -2)), list(range(count - 2, -1, -2))
    *sent, phi, plo = rhs_blocks(table, send_slots, (m, m_far, corange_test), parts, count)
    *sent, g, g_got = tie(*sent, g, g_got)
    g_parts = z_parts(g + g_got)
    kept = list(rhs_blocks(table, keep_slots, (phi, plo), parts, count))
    terms, tables = [], ()
    for k, slot in enumerate(keep_slots):
        got = to_y(sent[k])
        if slot == 0:
            terms += [kept[k], got]
            continue
        total = kept[k] + got
        if slot == 2 and tables:
            total, *tables = tie(total, *tables)
        terms.append(swap("space", slot)(total))
        if slot == 6:
            *g_parts, _ = tie(*g_parts, total)
        if slot == 2:
            g = z_sum(g_parts)
            g_far = to_core(g)
            m, g, g_far, _ = tie(m, g, g_far, total)
            tables = factor_start(table, g, g_far, m, m_far)
    if not tables:
        g = z_sum(g_parts)
        tables = factor_start(table, g, to_core(g), m, m_far)
    bit = count
    while bit < spaces:
        mine_sum = functools.reduce(jnp.add, terms)
        terms = [mine_sum, swap("space", bit)(mine_sum)]
        bit *= 2
    s2 = to_x(s0)
    s13 = to_core(jnp.concatenate([s0, s2], axis=0))

    upper, inverse, inverse_normal = factor_end(*tables)
    z0 = solve(inverse_normal, terms)

    blocks = {0: z0, 1: to_y(z0)}
    for slot in range(2, count, 2):
        blocks[slot] = swap("space", slot)(z0)
    for slot in range(2, count, 2):
        blocks[slot + 1] = to_y(blocks[slot])

    left, sparts, uparts, *done = outputs(
        table, [0, 1, 2][:count], scale, (s0, s2, s13, upper, inverse), field, [blocks[k] for k in range(min(3, count))])
    for slots in ([4, 6, 3], [5, 7]):
        if count > max(slots):
            done = outputs(table, slots, None, (sparts, uparts), field, [blocks[k] for k in slots], tuple(done))
    return (left, *done)


def solution(mesh):
    return jax.shard_map(
        per_device,
        mesh=mesh,
        in_specs=(P("space", "tm"), P("tm", None), P(None, "space")),
        out_specs=(P("space", None), P(None, "tm"), P("space", "tm")),
        check_vma=False,
    )
```

```python
import functools

import jax
import jax.numpy as jnp
from jax import lax
from jax.experimental import pallas as pl
from jax.experimental.pallas import tpu as pltpu
from jax.sharding import PartitionSpec as P

F32 = jnp.float32
BF16 = jnp.bfloat16
VMEM = pl.BlockSpec(memory_space=pltpu.VMEM)
SMEM = pl.BlockSpec(memory_space=pltpu.SMEM)
PANEL = 64
HBM = pl.BlockSpec(memory_space=pltpu.HBM)

CORE, MINE, TM = 8, 9, 10


def params(mib):
    return pltpu.CompilerParams(vmem_limit_bytes=mib * 2**20)


def exact(a, b, dims):
    return lax.dot_general(
        a, b, (dims, ((), ())), precision=lax.Precision.HIGHEST, preferred_element_type=F32
    )


def split(x):
    hi = x.astype(BF16)
    return hi, (x - hi.astype(F32)).astype(BF16)


def three(a, b, dims=((1,), (0,))):
    def one(x, y):
        return lax.dot_general(x, y, (dims, ((), ())), preferred_element_type=F32)

    return one(a[0], b[0]) + (one(a[0], b[1]) + one(a[1], b[0]))


def cost(macs, moved):
    return pl.CostEstimate(flops=macs // 8, bytes_accessed=moved // 16, transcendentals=0)


def pick(table, slots, i):
    slot = slots[-1]
    for k in range(len(slots) - 1):
        slot = jnp.where(i == k, slots[k], slot)
    return table[slot]


def shape(*dims, dtype=F32):
    return jax.ShapeDtypeStruct(dims, dtype)


def sketch_kernel(table, field, test, corange, s_send, s_keep, m_send, m_keep, fhi, flo, f, t, om, total, sems):
    cells, times = field.shape
    steps = f.shape[0]
    rows = cells // steps
    starts = [pl.multiple_of((table[TM] ^ slot) * rows, 128) for slot in (1, 3, 2, 0)]
    first = pltpu.make_async_copy(test, t, sems.at[steps])
    second = pltpu.make_async_copy(corange, om, sems.at[steps + 1])
    blocks = [pltpu.make_async_copy(field.at[pl.ds(at, rows), :], f.at[i], sems.at[i]) for i, at in enumerate(starts)]
    first.start()
    blocks[0].start()
    second.start()
    for block in blocks[1:]:
        block.start()
    first.wait()
    right = split(t[...])
    for i, at in enumerate(starts):
        blocks[i].wait()
        left = split(f[i])
        fhi[pl.ds(at, rows), :], flo[pl.ds(at, rows), :] = left
        s = three(left, right)
        out, half = (s_send, s_keep)[i // 2], i % 2
        out[half * rows:(half + 1) * rows, :] = s
        if i == 0:
            second.wait()
        part = three(split(om[:, pl.ds(at, rows)]), split(s))
        if i == 0:
            total[...] = part
        else:
            total[...] += part
    part = total.shape[0] // 8
    for out, slots in ((m_send, (1, 5, 3, 7)), (m_keep, (0, 4, 2, 6))):
        for j, k in enumerate(slots):
            at = pl.multiple_of((table[MINE] ^ k) * part, 8)
            out[j * part:(j + 1) * part, :] = total[pl.ds(at, part), :]


def sketches(table, field, test, corange):
    cells, times = field.shape
    rank = test.shape[1]
    steps = 4
    wide = corange.shape[0]
    anywhere = pl.BlockSpec(memory_space=pl.ANY)
    return pl.pallas_call(
        sketch_kernel,
        in_specs=[SMEM] + [anywhere] * 3,
        out_specs=[VMEM] * 6,
        scratch_shapes=[
            pltpu.VMEM((steps, cells // steps, times), F32),
            pltpu.VMEM((times, rank), F32),
            pltpu.VMEM((wide, cells), F32),
            pltpu.VMEM((wide, rank), F32),
            pltpu.SemaphoreType.DMA((steps + 2,)),
        ],
        out_shape=[shape(cells // 2, rank)] * 2 + [shape(wide // 2, rank)] * 2 + [shape(cells, times, dtype=BF16)] * 2,
        compiler_params=params(52),
        cost_estimate=cost(3 * cells * rank * (times + wide), 4 * cells * times),
        name="sketches",
    )(table, field, test, corange)


def gram_kernel(table, a, b, s, g_send, g_keep, total):
    x = a[...] + b[...]
    s[...] = x
    total[...] = exact(x, x, ((0,), (0,)))
    rows = total.shape[0] // 2
    me = table[CORE]
    g_keep[...] = total[pl.ds(pl.multiple_of(me * rows, 8), rows), :]
    g_send[...] = total[pl.ds(pl.multiple_of((1 - me) * rows, 8), rows), :]


def gram_of(table, a, b):
    rank = a.shape[1]
    return pl.pallas_call(
        gram_kernel,
        out_shape=[shape(*a.shape), shape(rank // 2, rank), shape(rank // 2, rank)],
        in_specs=[SMEM, VMEM, VMEM],
        out_specs=[VMEM] * 3,
        scratch_shapes=[pltpu.VMEM((rank, rank), F32)],
        compiler_params=params(8),
        cost_estimate=cost(6 * a.shape[0] * rank * rank, 12 * a.shape[0] * rank),
        name="gram",
    )(table, a, b)


ORDER = (0, 4, 2, 6, 1, 5, 3, 7)


def stack_rows(parts):
    return jnp.concatenate([parts[0], parts[1], parts[0]], axis=0)


def rhs_kernel(slots, first, table, *refs):
    if first:
        near, far, corange, fhi, flo = refs[:5]
        outs, (phi, plo, m, om) = refs[5:-4], refs[-4:]
        half = near.shape[0]
        rows = half // 4
        m[:half] = near[...]
        m[half:] = far[...]
        for j, slot in enumerate(ORDER):
            at = pl.multiple_of((table[MINE] ^ slot) * rows, 8)
            om[j * rows:(j + 1) * rows, :] = corange[pl.ds(at, rows), :]
        phi[...], plo[...] = split(three(split(m[...].T), split(om[...])))
    else:
        phi, plo, fhi, flo = refs[:4]
        outs = refs[4:]
    cols = outs[0].shape[1]
    for k, slot in enumerate(slots):
        at = pl.ds(pl.multiple_of(table[slot] * cols, 128), cols)
        outs[k][...] = three((phi[...], plo[...]), (fhi[:, at], flo[:, at]))


def rhs_blocks(table, slots, operands, parts, blocks):
    count = len(slots)
    first = len(operands) > 2
    rank = operands[0].shape[1] if first else operands[0].shape[0]
    cells, times = parts[0].shape
    cols = times // blocks
    wide = operands[2].shape[0] if first else 0
    return pl.pallas_call(
        functools.partial(rhs_kernel, slots, first),
        in_specs=[SMEM] + [VMEM] * (len(operands) + 2),
        out_specs=[VMEM] * (count + 2 * first),
        scratch_shapes=[pltpu.VMEM((wide, rank), F32), pltpu.VMEM((wide, cells), F32)] * first,
        out_shape=[shape(rank, cols)] * count + [shape(rank, cells, dtype=BF16)] * (2 * first),
        compiler_params=params(20),
        cost_estimate=cost(3 * count * rank * cells * cols, 4 * count * cells * cols),
        name="rhs",
    )(table, *operands, *parts)


def eliminate(blocks):
    width = blocks[0].shape[1]
    groups = PANEL // 8
    mats = [[x[8 * g:8 * g + 8] for g in range(groups)] for x in blocks]
    row = lax.broadcasted_iota(jnp.int32, (8, width), 0)
    for s in range(groups):
        columns = [
            {
                g: [jnp.broadcast_to(m[g][:, 8 * s + j:8 * s + j + 1], (8, width)) for j in range(8)]
                for g in range(s, groups)
            }
            for m in mats
        ]
        for i in range(8):
            for m, c in zip(mats, columns):
                inverse = 1.0 / c[s][i][i:i + 1]
                below = {g: c[g][i] for g in range(s, groups)}
                below[s] = jnp.where(row > i, below[s], 0.0)
                for j in range(i + 1, 8):
                    f = c[s][j][i:i + 1] * inverse
                    for g in range(s, groups):
                        c[g][j] = c[g][j] - below[g] * f
                u = m[s][i:i + 1] * inverse
                for g in range(s, groups):
                    m[g] = m[g] - below[g] * u
    return mats


def iotas(dims):
    return lax.broadcasted_iota(jnp.int32, dims, 0), lax.broadcasted_iota(jnp.int32, dims, 1)


def factor_both(n, tables, panels):
    r, c = iotas((PANEL, PANEL))
    eye = jnp.where(r == c, 1.0, 0.0)
    r, c = iotas((PANEL, 2 * PANEL))
    for k in panels:
        lo, hi = k * PANEL, (k + 1) * PANEL
        blocks = [jnp.concatenate([t[lo:hi, lo:hi], eye], axis=1) for t in tables]
        left = lo // 128 * 128
        right = n + (hi + 127) // 128 * 128
        rest = hi // 128 * 128
        for t, m in zip(tables, eliminate(blocks)):
            x = jnp.concatenate(m, axis=0)
            pivots = jnp.sum(jnp.where(r == c, x, 0.0), axis=1, keepdims=True)
            inverse = (x * lax.rsqrt(pivots))[:, PANEL:]
            panel = exact(inverse, t[lo:hi, left:right], ((1,), (0,)))
            if hi < n:
                update = exact(panel[:, rest - left:n - left], panel[:, rest - left:], ((0,), (0,)))
                t[hi:n, rest:right] = t[hi:n, rest:right] - update[hi - rest:]
            t[lo:hi, left:right] = panel


def factor_head(panels, table, g_near, g_far, m_near, m_far, t1, t2):
    n = g_near.shape[1]
    half = n // 2
    r, c = iotas((n, n))
    eye = jnp.where(r == c, 1.0, 0.0)
    me = table[CORE]
    t1[pl.ds(pl.multiple_of(me * half, 8), half), :n] = g_near[...]
    t1[pl.ds(pl.multiple_of((1 - me) * half, 8), half), :n] = g_far[...]
    t1[:, n:] = eye
    t2[:, :n] = exact(m_near[...], m_near[...], ((0,), (0,))) + exact(m_far[...], m_far[...], ((0,), (0,)))
    t2[:, n:] = eye
    factor_both(n, (t1, t2), panels)


def factor_tail(panels, head1, head2, upper, inverse, normal_inverse, t1, t2):
    n = upper.shape[0]
    t1[...] = head1[...]
    t2[...] = head2[...]
    factor_both(n, (t1, t2), panels)
    r, c = iotas((n, n))
    upper[...] = jnp.where(r <= c, t1[:, :n], 0.0)
    inverse[...] = t1[:, n:]
    k = t2[:, n:]
    normal_inverse[...] = exact(k, k, ((0,), (0,)))


def factor_start(table, g_near, g_far, m_near, m_far):
    n = g_near.shape[1]
    return pl.pallas_call(
        functools.partial(factor_head, range(n // PANEL // 2)),
        out_shape=[shape(n, 2 * n)] * 2,
        in_specs=[SMEM] + [VMEM] * 4,
        out_specs=[VMEM] * 2,
        compiler_params=params(16),
        cost_estimate=cost(3 * 10**9, 4 * n * n * 8),
        name="factor",
    )(table, g_near, g_far, m_near, m_far)


def factor_end(t1, t2):
    n = t1.shape[0]
    return pl.pallas_call(
        functools.partial(factor_tail, range(n // PANEL // 2, n // PANEL)),
        out_shape=[shape(n, n)] * 3,
        in_specs=[VMEM] * 2,
        out_specs=[VMEM] * 3,
        scratch_shapes=[pltpu.VMEM((n, 2 * n), F32)] * 2,
        compiler_params=params(16),
        cost_estimate=cost(3 * 10**9, 4 * n * n * 8),
        name="factor",
    )(t1, t2)


def solve_kernel(projector, *refs):
    total = refs[0][...]
    for ref in refs[1:-1]:
        total += ref[...]
    refs[-1][...] = three(split(projector[...]), split(total))


def solve(projector, terms):
    return pl.pallas_call(
        solve_kernel,
        out_shape=shape(projector.shape[0], terms[0].shape[1]),
        in_specs=[VMEM] * (len(terms) + 1),
        out_specs=VMEM,
        compiler_params=params(16),
        cost_estimate=cost(3 * projector.shape[0] * terms[0].size, 4 * terms[0].size * (len(terms) + 2)),
        name="solve",
    )(projector, *terms)


def output_kernel(slots, scale, table, *refs):
    count = len(slots)
    first = scale is not None
    i = pl.program_id(0)
    if first:
        s0, s2, s13, upper, inverse, field = refs[:6]
        blocks = refs[6:6 + count]
        left, sparts, uparts, right, residual, z = refs[6 + count:]
        rows, rank = s0.shape

        @pl.when(i == 0)
        def _():
            uparts[:, :rank], uparts[:, 2 * rank:] = split(upper[...])
            uparts[:, rank:2 * rank] = uparts[:, :rank]
            inv = split(inverse[...])
            for slot, ref, start in ((0, s0, 0), (2, s2, 0), (1, s13, 0), (3, s13, rows)):
                at = pl.ds(pl.multiple_of((table[TM] ^ slot) * rows, 16), rows)
                hi, lo = split(ref[start:start + rows, :])
                sparts[at, :rank] = hi
                sparts[at, rank:2 * rank] = hi
                sparts[at, 2 * rank:] = lo
                left[at, :] = three((hi, lo), inv, ((1,), (1,))) * scale
    else:
        sparts, uparts, field = refs[:3]
        blocks = refs[3:3 + count]
        right, residual, z = refs[5 + count:]

    for k in range(count):
        @pl.when(i == k)
        def _():
            z[...] = stack_rows(split(blocks[k][...]))

    right[...] = jnp.dot(uparts[...], z[...], preferred_element_type=F32)
    residual[...] = field[...] - jnp.dot(sparts[...], z[...], preferred_element_type=F32)


def outputs(table, slots, scale, operands, field, blocks, before=()):
    cells, times = field.shape
    rank, cols = blocks[0].shape
    count = len(slots)
    first = scale is not None
    whole = lambda *dims: pl.BlockSpec(dims, lambda i, p: (0,) * len(dims))
    ahead = 1 + len(operands) + 1 + count
    return pl.pallas_call(
        functools.partial(output_kernel, slots, scale),
        grid_spec=pltpu.PrefetchScalarGridSpec(
            num_scalar_prefetch=1,
            grid=(count,),
            in_specs=[whole(*x.shape) for x in operands]
            + [pl.BlockSpec((cells, cols), lambda i, p: (0, pick(p, slots, i)))]
            + [whole(rank, cols)] * count
            + [pl.BlockSpec(memory_space=pl.ANY)] * len(before),
            out_specs=[whole(cells, rank), whole(cells, 3 * rank), whole(rank, 3 * rank)] * first + [
                pl.BlockSpec((rank, cols), lambda i, p: (0, pick(p, slots, i))),
                pl.BlockSpec((cells, cols), lambda i, p: (0, pick(p, slots, i))),
            ],
            scratch_shapes=[pltpu.VMEM((3 * rank, cols), BF16)],
        ),
        out_shape=[shape(cells, rank), shape(cells, 3 * rank, dtype=BF16), shape(rank, 3 * rank, dtype=BF16)] * first
        + [shape(rank, times), shape(cells, times)],
        input_output_aliases={} if first else {ahead: 0, ahead + 1: 1},
        compiler_params=params(36),
        cost_estimate=cost(3 * cells * rank * cols * count, 8 * cells * cols * count),
        name="outputs",
    )(table, *operands, field, *blocks, *before)


def swap(axis, bit):
    n = lax.axis_size(axis)

    def go(x):
        return lax.ppermute(x, axis, [(i, i ^ bit) for i in range(n)])

    return go


def tie(*arrays):
    return lax.optimization_barrier(arrays)


def z_parts(v):
    return [v] + [swap("space", bit)(v) for bit in (2, 4, 6)] if lax.axis_size("space") >= 8 else [v]


def z_sum(parts):
    spaces = lax.axis_size("space")
    v, bit = parts[0], 2
    if len(parts) > 1:
        v, bit = (v + parts[1]) + (parts[2] + parts[3]), 8
    while bit < spaces:
        v = v + swap("space", bit)(v)
        bit *= 2
    return v


def per_device(field, range_test, corange_test):
    spaces, tms = lax.axis_size("space"), lax.axis_size("tm")
    space, tm = lax.axis_index("space"), lax.axis_index("tm")
    scale = float(field.shape[0] * spaces) ** 0.5
    core, y, x = tm & 1, space & 1, (tm >> 1) & 1
    to_core, to_x = swap("tm", 1), swap("tm", 2)
    to_y = swap("space", 1)

    def to_xy(v):
        pairs = [(s * tms + t, (s ^ 1) * tms + (t ^ 2)) for s in range(spaces) for t in range(tms)]
        return lax.ppermute(v, ("space", "tm"), pairs)


    count = min(spaces, 8)
    near = space & (count - 1)
    mine = core | (y << 1) | (x << 2)
    numbers = jnp.array([core, mine, tm])
    table = jnp.concatenate([near ^ jnp.arange(8, dtype=jnp.int32), numbers]).astype(jnp.int32)

    s_send, s_keep, m_send, m_keep, *parts = sketches(table, field, range_test, corange_test)
    quarter = s_keep.shape[0] // 2

    m = m_keep + to_core(m_send)
    got = to_core(s_send)
    s_far, s_near = s_keep[:quarter] + got[quarter:], s_keep[quarter:] + got[:quarter]
    m, s_far, s_near = tie(m, s_far, s_near)
    rows = m.shape[0] // 4
    k0, kx, ky, kxy = (m[i * rows:(i + 1) * rows] for i in range(4))
    s_x = to_x(s_far)
    m = (k0 + to_x(kx)) + (to_y(ky) + to_xy(kxy))
    s_x, _ = tie(s_x, m)
    s0, g_send, g = gram_of(table, s_near, s_x)
    g_got = to_core(g_send)
    m = z_sum(z_parts(m))
    m, g, g_got = tie(m, g, g_got)
    g = g + g_got
    g_got = to_x(g)
    m = jnp.concatenate([m, to_x(m), to_y(m), to_xy(m)], axis=0)
    g, g_got, _ = tie(g, g_got, m)
    g = g + g_got
    m_far = to_core(m)
    g_got = to_y(g)

    send_slots, keep_slots = list(range(count - 1, 0, -2)), list(range(count - 2, -1, -2))
    *sent, phi, plo = rhs_blocks(table, send_slots, (m, m_far, corange_test), parts, count)
    *sent, g, g_got = tie(*sent, g, g_got)
    g_parts = z_parts(g + g_got)
    kept = list(rhs_blocks(table, keep_slots, (phi, plo), parts, count))
    terms, tables = [], ()
    for k, slot in enumerate(keep_slots):
        got = to_y(sent[k])
        if slot == 0:
            terms += [kept[k], got]
            continue
        total = kept[k] + got
        if slot == 2 and tables:
            total, *tables = tie(total, *tables)
        terms.append(swap("space", slot)(total))
        if slot == 6:
            *g_parts, _ = tie(*g_parts, total)
        if slot == 2:
            g = z_sum(g_parts)
            g_far = to_core(g)
            m, g, g_far, _ = tie(m, g, g_far, total)
            tables = factor_start(table, g, g_far, m, m_far)
    if not tables:
        g = z_sum(g_parts)
        tables = factor_start(table, g, to_core(g), m, m_far)
    bit = count
    while bit < spaces:
        mine_sum = functools.reduce(jnp.add, terms)
        terms = [mine_sum, swap("space", bit)(mine_sum)]
        bit *= 2
    s2 = to_x(s0)
    s13 = to_core(jnp.concatenate([s0, s2], axis=0))

    upper, inverse, inverse_normal = factor_end(*tables)
    z0 = solve(inverse_normal, terms)

    blocks = {0: z0, 1: to_y(z0)}
    for slot in range(2, count, 2):
        blocks[slot] = swap("space", slot)(z0)
    for slot in range(2, count, 2):
        blocks[slot + 1] = to_y(blocks[slot])

    left, sparts, uparts, *done = outputs(
        table, [0, 1, 2][:count], scale, (s0, s2, s13, upper, inverse), field, [blocks[k] for k in range(min(3, count))])
    for slots in ([4, 6, 3], [5, 7]):
        if count > max(slots):
            done = outputs(table, slots, None, (sparts, uparts), field, [blocks[k] for k in slots], tuple(done))
    return (left, *done)


def solution(mesh):
    return jax.shard_map(
        per_device,
        mesh=mesh,
        in_specs=(P("space", "tm"), P("tm", None), P(None, "space")),
        out_specs=(P("space", None), P(None, "tm"), P("space", "tm")),
        check_vma=False,
    )
```
